128 devices in a mesh: row: 16 (over z, y_lo, core), col: 8 (over x, y_hi).
Axes of the slice: x: 4, y: 4 (y_hi: 2, y_lo: 2; y = y_hi * 2 + y_lo), z: 4, core: 2. Of those that a mesh axis runs over, the one named last changes fastest.
Arguments:
- pair: bfloat16 [512, 512, 128], P('row', 'col'), may hold values from -6 to 6
- mask: int32 [512], replicated, may hold values 0 or 1
- out_in: bfloat16 [128, 512], replicated, may hold values from -0.5 to 0.5
- out_gate: bfloat16 [128, 128], replicated, may hold values from -0.5 to 0.5
- out_final: bfloat16 [128, 128], replicated, may hold values from -0.5 to 0.5
- in_in: bfloat16 [128, 512], replicated, may hold values from -0.5 to 0.5
- in_gate: bfloat16 [128, 128], replicated, may hold values from -0.5 to 0.5
- in_final: bfloat16 [128, 128], replicated, may hold values from -0.5 to 0.5
Outputs:
- updated: bfloat16 [512, 512, 128], P('row', 'col')
The draws below stay inside these ranges and needn't reach their ends.
All inputs are finite; a program needn't handle non-finite values.
Results may differ from the reference program's by a relative error of at most 0.009.
Values may be sent and summed in bfloat16 or wider, within the bound.
A program may use at most 128 MiB of HBM per device.

```python
import jax
import jax.numpy as jnp
from jax import lax

CH = 128
NRES = 512


def place_ends(result, rng, low, largest):
    longest = result.shape.index(max(result.shape))
    spots = []
    for shift in (0, 1):
        where = [jax.random.randint(jax.random.fold_in(rng, axis), (), 0, length) for axis, length in enumerate(result.shape)]
        where[longest] = (where[longest] + shift) % result.shape[longest]
        spots.append(tuple(where))
    return result.at[spots[0]].set(low).at[spots[1]].set(largest)


def block_scale(stream_key, extent, shards, low, top_value):
    gain = 1.0
    for dim, blocks in shards:
        steps = jax.random.uniform(jax.random.fold_in(jax.random.fold_in(stream_key, 6), dim), (blocks,), jnp.float32, low / len(shards), top_value / len(shards))
        gain = gain * jnp.repeat(jnp.exp(steps), extent[dim] // blocks).reshape((-1,) + (1,) * (len(extent) - 1 - dim))
    return gain


def scatter_about(key, extent, scale, bound, shards=(), kind=jnp.bfloat16):
    drawn = scale * jax.random.normal(key, extent, jnp.float32)
    if shards:
        drawn = drawn * block_scale(key, extent, shards, -0.22, 0.18)
    return jnp.clip(drawn, -bound, bound).astype(kind)


def setup_inputs(seed: int = 0) -> dict:
    splits = jax.random.split(jax.random.key(seed), 9)
    return {
        "pair": scatter_about(splits[0], (NRES, NRES, CH), 1.0, 6.0, ((0, 16), (1, 8))),
        "mask": place_ends((jax.random.randint(splits[1], (NRES,), 0, 8) < 7).astype(jnp.int32), jax.random.fold_in(splits[1], 1), 0, 1),
        "out_in": scatter_about(splits[2], (CH, 4 * CH), CH ** -0.5, 0.5),
        "out_gate": scatter_about(splits[3], (CH, CH), CH ** -0.5, 0.5),
        "out_final": scatter_about(splits[4], (CH, CH), CH ** -0.5, 0.5),
        "in_in": scatter_about(splits[5], (CH, 4 * CH), CH ** -0.5, 0.5),
        "in_gate": scatter_about(splits[6], (CH, CH), CH ** -0.5, 0.5),
        "in_final": scatter_about(splits[7], (CH, CH), CH ** -0.5, 0.5),
    }


def normalize(values):
    center = values - lax.optimization_barrier(jnp.mean(values, axis=-1, keepdims=True))
    spread = lax.optimization_barrier(jnp.mean(center * center, axis=-1, keepdims=True))
    return center * lax.rsqrt(spread + 1e-05)

def branch_inputs(tile, w_in, w_gate, pair_mask):
    normed = normalize(tile.astype(jnp.float32)).astype(jnp.bfloat16)
    proj = jnp.einsum('ijc,cd->ijd', normed.astype(jnp.float32), w_in.astype(jnp.float32))
    width = w_gate.shape[0]
    weight = pair_mask[:, :, None]
    left = (weight * jax.nn.sigmoid(proj[..., 0:width]) * proj[..., width:2 * width]).astype(jnp.bfloat16)
    right = (weight * jax.nn.sigmoid(proj[..., 2 * width:3 * width]) * proj[..., 3 * width:4 * width]).astype(jnp.bfloat16)
    gate = jax.nn.sigmoid(jnp.einsum('ijc,cd->ijd', normed.astype(jnp.float32), w_gate.astype(jnp.float32)))
    return (left, right, gate)

def finish(tile, total, gate, w_final):
    shaped = normalize(total).astype(jnp.bfloat16)
    branch = jnp.einsum('ijc,cd->ijd', shaped.astype(jnp.float32), w_final.astype(jnp.float32))
    return (tile.astype(jnp.float32) + gate * branch).astype(jnp.bfloat16)

def reference(pair, mask, out_in, out_gate, out_final, in_in, in_gate, in_final):
    weights = mask.astype(jnp.float32)
    pair_mask = weights[:, None] * weights[None, :]
    left, right, gate = branch_inputs(pair, out_in, out_gate, pair_mask)
    total = jnp.einsum('ikc,jkc->ijc', left.astype(jnp.float32), right.astype(jnp.float32))
    middle = finish(pair, total, gate, out_final)
    left, right, gate = branch_inputs(middle, in_in, in_gate, pair_mask)
    total = jnp.einsum('kic,kjc->ijc', left.astype(jnp.float32), right.astype(jnp.float32))
    return finish(middle, total, gate, in_final)
```

```python
import functools

import jax
import jax.numpy as jnp
from jax import lax
from jax.experimental import pallas as pl
from jax.experimental.pallas import tpu as pltpu
from jax.sharding import PartitionSpec as P

MESH = pl.DeviceIdType.MESH
CH = 128
S = 16
L = 128
DEVS = 128
ROWS = 16
COLS = 8
SCRAMBLE = 37
BF = jnp.bfloat16
F32 = jnp.float32


def place(t):
    row, col = lax.axis_index("row"), lax.axis_index("col")
    x = lax.rem(col // 2 + lax.rem(t // 2, 4), 4)
    y = lax.rem(lax.rem(col, 2) * 2 + lax.rem(row // 2, 2) + lax.rem(t // 8, 4), 4)
    z = lax.rem(row // 4 + t // 32, 4)
    core = lax.rem(lax.rem(row, 2) + lax.rem(t, 2), 2)
    to_row = z * 4 + lax.rem(y, 2) * 2 + core
    to_col = x * 2 + y // 2
    return to_row, to_col, to_row * COLS + to_col


def sigmoid(v):
    return 0.5 * jnp.tanh(0.5 * v) + 0.5


def norm0(v):
    center = v - jnp.mean(v, axis=0, keepdims=True)
    spread = jnp.mean(center * center, axis=0, keepdims=True)
    return center * lax.rsqrt(spread + 1e-05)


def swap_halves(first, second):
    low = lax.broadcasted_iota(jnp.int32, first.shape, 1) < 64
    return (
        jnp.where(low, first, pltpu.roll(second, 64, 1)),
        jnp.where(low, pltpu.roll(first, 64, 1), second),
    )


def exchange(send, recv, sems, me):
    send_sem, recv_sem = sems

    @pl.loop(1, DEVS)
    def _(t):
        to_row, to_col, to = place(lax.rem(t * SCRAMBLE, DEVS))
        pltpu.make_async_remote_copy(
            src_ref=send.at[to],
            dst_ref=recv.at[me],
            send_sem=send_sem,
            recv_sem=recv_sem,
            device_id=(to_row, to_col),
            device_id_type=MESH,
        ).start()

    recv[me] = send[me]


def arrived(send, recv, sems):
    others = pl.ds(0, DEVS - 1)
    pltpu.make_async_copy(recv.at[others], recv.at[others], sems[1]).wait()


def sent(send, recv, sems):
    others = pl.ds(0, DEVS - 1)
    pltpu.make_async_copy(send.at[others], send.at[others], sems[0]).wait()


def branch_inputs(q, values, weights, mask, gate, left, right):
    normed = norm0(values).astype(BF)
    proj = jnp.dot(weights[...], normed, preferred_element_type=F32)
    keep = jnp.concatenate([mask[pl.ds(2 * q, 1), :], mask[pl.ds(2 * q + 1, 1), :]], axis=1)
    lv = keep * sigmoid(proj[0:CH]) * proj[CH : 2 * CH]
    rv = keep * sigmoid(proj[2 * CH : 3 * CH]) * proj[3 * CH : 4 * CH]
    gate[q] = sigmoid(proj[4 * CH : 5 * CH])
    for e in range(2):
        rows = pl.ds(2 * q + e, CH, stride=S)
        left[rows, :] = lv[:, e * L : (e + 1) * L]
        right[rows, :] = rv[:, e * L : (e + 1) * L]


def pack(left, right, send):
    @pl.loop(0, CH // 16)
    def _(g):
        rows = pl.ds(pl.multiple_of(g * 256, 256), 256)
        chans = pl.ds(g * 16, 16)
        send[chans, 0:S, :] = left[rows, :].reshape(16, S, L).astype(BF)
        send[chans, S : 2 * S, :] = right[rows, :].reshape(16, S, L).astype(BF)


def multiply(recv, lmat, rmat, send, dims):
    @pl.loop(0, ROWS)
    def _(r):
        for part, mat in ((0, lmat), (1, rmat)):
            for p in range(COLS // 2):
                first = recv[r * COLS + 2 * p, part * S : (part + 1) * S, :]
                second = recv[r * COLS + 2 * p + 1, part * S : (part + 1) * S, :]
                low, high = swap_halves(first, second)
                at = pl.multiple_of(r * 2 * S, 2 * S)
                mat[pl.ds(at, S), p * L : (p + 1) * L] = low
                mat[pl.ds(at + S, S), p * L : (p + 1) * L] = high

    for block in range(4):
        rows = slice(block * 128, (block + 1) * 128)
        part = lmat[rows, :] if dims == 1 else lmat[:, rows]
        total = lax.dot_general(
            part, rmat[...], (((dims,), (dims,)), ((), ())), preferred_element_type=F32
        ).astype(BF)
        for k in range(4):
            r = block * 4 + k
            for p in range(COLS // 2):
                cols = slice(p * L, (p + 1) * L)
                low, high = swap_halves(
                    total[k * 2 * S : k * 2 * S + S, cols], total[k * 2 * S + S : (k + 1) * 2 * S, cols]
                )
                send[r * COLS + 2 * p] = low
                send[r * COLS + 2 * p + 1] = high


def shape(recv, wide):
    total = jnp.zeros((S, L), F32)
    total = lax.fori_loop(0, 8, lambda g, a: a + jnp.sum(recv[pl.ds(g * 16, 16)].astype(F32), axis=0), total)
    mean = total * (1.0 / CH)

    def squares(g, a):
        center = recv[pl.ds(g * 16, 16)].astype(F32) - mean[None]
        return a + jnp.sum(center * center, axis=0)

    spread = lax.fori_loop(0, 8, squares, jnp.zeros((S, L), F32)) * (1.0 / CH)
    scale = lax.rsqrt(spread + 1e-05)

    @pl.loop(0, 8)
    def _(g):
        rows = pl.ds(pl.multiple_of(g * 256, 256), 256)
        wide[rows, :] = ((recv[pl.ds(g * 16, 16)].astype(F32) - mean[None]) * scale[None]).reshape(256, L)


def finish(q, wide, weights, gate, base):
    shaped = jnp.concatenate(
        [wide[pl.ds(2 * q + e, CH, stride=S), :] for e in range(2)], axis=1
    ).astype(BF)
    branch = jnp.dot(weights[...], shaped, preferred_element_type=F32)
    return (base[q].astype(F32) + gate[q] * branch).astype(BF)


def kernel(
    pair, mask, in1, gate1, final1, in2, gate2, final2, out,
    base, gate, left, right, wt, ft, keep,
    send_a, recv_a, send_b, recv_b, send_c, recv_c, send_d, recv_d, lmat, rmat, send_sems, recv_sems,
):
    row, col = lax.axis_index("row"), lax.axis_index("col")
    me = row * COLS + col
    sems = [(send_sems.at[k], recv_sems.at[k]) for k in range(4)]

    barrier = pltpu.get_barrier_semaphore()

    @pl.loop(1, DEVS)
    def _(t):
        to_row, to_col, _ = place(t)
        pl.semaphore_signal(barrier, inc=1, device_id=(to_row, to_col), device_id_type=MESH)

    for k, (a, b, c) in enumerate(((in1, gate1, final1), (in2, gate2, final2))):
        wt[k, 0 : 4 * CH] = a[...].astype(F32).T.astype(BF)
        wt[k, 4 * CH : 5 * CH] = b[...].astype(F32).T.astype(BF)
        ft[k] = c[...].astype(F32).T.astype(BF)

    held = mask[...].astype(F32)
    spot = lax.broadcasted_iota(jnp.int32, (S, 512), 1)
    line = lax.broadcasted_iota(jnp.int32, (S, 512), 0)
    first = jnp.sum(jnp.where(spot == row * 32 + line, held, 0.0), axis=1, keepdims=True)
    second = jnp.sum(jnp.where(spot == row * 32 + 16 + line, held, 0.0), axis=1, keepdims=True)
    spot = lax.broadcasted_iota(jnp.int32, (L, 512), 1)
    line = lax.broadcasted_iota(jnp.int32, (L, 512), 0)
    across = jnp.sum(
        jnp.where(spot == col * 64 + lax.rem(line, 64), held, 0.0), axis=1, keepdims=True
    )
    across = jnp.broadcast_to(across, (L, L)).T[0:S]
    lane = lax.broadcasted_iota(jnp.int32, (S, L), 1)
    keep[...] = jnp.where(lane < 64, first, second) * across

    @pl.loop(0, S // 2)
    def _(q):
        values = jnp.concatenate(
            [pair[2 * q], pair[S + 2 * q], pair[2 * q + 1], pair[S + 2 * q + 1]], axis=0
        )
        values = values.astype(F32).T
        base[q] = values.astype(BF)
        branch_inputs(q, values, wt.at[0], keep, gate, left, right)

    pack(left, right, send_a)
    pl.semaphore_wait(barrier, DEVS - 1)
    exchange(send_a, recv_a, sems[0], me)
    arrived(send_a, recv_a, sems[0])
    multiply(recv_a, lmat, rmat, send_b, 1)
    exchange(send_b, recv_b, sems[1], me)
    arrived(send_b, recv_b, sems[1])
    shape(recv_b, left)

    @pl.loop(0, S // 2)
    def _(q):
        middle = finish(q, left, ft.at[0], gate, base)
        base[q] = middle
        branch_inputs(q, middle.astype(F32), wt.at[1], keep, gate, left, right)

    pack(left, right, send_c)
    exchange(send_c, recv_c, sems[2], me)
    arrived(send_c, recv_c, sems[2])
    multiply(recv_c, lmat, rmat, send_d, 0)
    exchange(send_d, recv_d, sems[3], me)
    arrived(send_d, recv_d, sems[3])
    shape(recv_d, left)

    @pl.loop(0, S // 2)
    def _(q):
        done = finish(q, left, ft.at[1], gate, base).astype(F32).T.astype(BF)
        out[2 * q] = done[0:64]
        out[S + 2 * q] = done[64:128]
        out[2 * q + 1] = done[128:192]
        out[S + 2 * q + 1] = done[192:256]

    for k, (a, b) in enumerate(((send_a, recv_a), (send_b, recv_b), (send_c, recv_c), (send_d, recv_d))):
        sent(a, b, sems[k])


def shards(pair, mask, *weights):
    vmem = pl.BlockSpec(memory_space=pltpu.VMEM)
    two = pltpu.VMEM((DEVS, 2 * S, L), BF)
    one = pltpu.VMEM((DEVS, S, L), BF)
    return pl.pallas_call(
        kernel,
        out_shape=jax.ShapeDtypeStruct(pair.shape, BF),
        in_specs=[vmem] * 8,
        out_specs=vmem,
        scratch_shapes=[
            pltpu.VMEM((S // 2, CH, 2 * L), BF),
            pltpu.VMEM((S // 2, CH, 2 * L), F32),
            pltpu.VMEM((CH * S, L), F32),
            pltpu.VMEM((CH * S, L), F32),
            pltpu.VMEM((2, 5 * CH, CH), BF),
            pltpu.VMEM((2, CH, CH), BF),
            pltpu.VMEM((S, L), F32),
            two, two, one, one, two, two, one, one,
            pltpu.VMEM((512, 512), BF),
            pltpu.VMEM((512, 512), BF),
            pltpu.SemaphoreType.DMA((4,)),
            pltpu.SemaphoreType.DMA((4,)),
        ],
        compiler_params=pltpu.CompilerParams(
            collective_id=0, has_side_effects=True, vmem_limit_bytes=48 * 2**20
        ),
    )(pair, mask.reshape(1, 512), *weights)


def solution(mesh):
    return jax.shard_map(
        shards,
        mesh=mesh,
        in_specs=(P("row", "col", None), P(), P(), P(), P(), P(), P(), P()),
        out_specs=P("row", "col", None),
        check_vma=False,
    )
```

```python
import jax
import jax.numpy as jnp
from jax import lax
from jax.experimental import pallas as pl
from jax.experimental.pallas import tpu as pltpu
from jax.sharding import PartitionSpec as P

VMEM_BYTES = 63 * 2**20
UNROLL = True
LOGICAL = pl.DeviceIdType.LOGICAL
CH = 128
S = 16
L = 128
DEVS = 128
ROWS = 16
COLS = 8
BF = jnp.bfloat16
F32 = jnp.float32
PLANE = sorted(
    ((dx, dy, dc) for dx in range(4) for dy in range(4) for dc in range(2)),
    key=lambda o: -min(o[0], 4 - o[0]) - min(o[1], 4 - o[1]),
)
ORDER = sorted(
    ((dx, dy, dz, dc) for dz in range(4) for dy in range(4) for dx in range(4) for dc in range(2)),
    key=lambda o: -sum(min(v, 4 - v) for v in o[:3]),
)[:-2] + [(0, 0, 0, 1)]


class Torus:
    def __init__(self):
        row, col = lax.axis_index("row"), lax.axis_index("col")
        self.me = row * COLS + col
        self.z = row // 4
        y = lax.rem(col, 2) * 2 + lax.rem(row // 2, 2)
        self.planes = [lax.rem(self.z + d, 4) for d in range(4)]
        ys = [lax.rem(y + d, 4) for d in range(4)]
        self.ys = [lax.rem(v, 2) * 16 + v // 2 for v in ys]
        self.xs = [lax.rem(col // 2 + d, 4) * 2 for d in range(4)]
        self.cs = [lax.rem(lax.rem(row, 2) + d, 2) * 8 for d in range(2)]

    def at(self, dx, dy, dz, dc):
        return self.planes[dz] * 32 + self.ys[dy] + self.xs[dx] + self.cs[dc]


def sigmoid(v):
    return 0.5 * jnp.tanh(0.5 * v) + 0.5


def norm0(v):
    center = v - jnp.mean(v, axis=0, keepdims=True)
    spread = jnp.mean(center * center, axis=0, keepdims=True)
    return center * lax.rsqrt(spread + 1e-05)


def swap_halves(first, second):
    low = lax.broadcasted_iota(jnp.int32, first.shape, 1) < 64
    return (
        jnp.where(low, first, pltpu.roll(second, 64, 1)),
        jnp.where(low, pltpu.roll(first, 64, 1), second),
    )


def push(torus, to, send, recv, sems):
    pltpu.make_async_remote_copy(
        src_ref=send.at[to],
        dst_ref=recv.at[torus.me],
        send_sem=sems[0],
        recv_sem=sems[1],
        device_id=to,
        device_id_type=LOGICAL,
    ).start()


def exchange(torus, send, recv, sems):
    for offset in ORDER:
        push(torus, torus.at(*offset), send, recv, sems)
    recv[torus.me] = send[torus.me]


def wait_all(ref, sem):
    others = ref.at[pl.ds(0, DEVS - 1)]
    pltpu.make_async_copy(others, others, sem).wait()


def edge(side, weights, normed, keep, wide, send):
    @pl.loop(0, S // 2, unroll=UNROLL)
    def _(q):
        proj = jnp.dot(
            weights[side * 2 * CH : (side + 1) * 2 * CH, :], normed[q], preferred_element_type=F32
        )
        mask = jnp.concatenate([keep[pl.ds(2 * q, 1), :], keep[pl.ds(2 * q + 1, 1), :]], axis=1)
        value = mask * sigmoid(proj[0:CH]) * proj[CH : 2 * CH]
        for e in range(2):
            wide[pl.ds(2 * q + e, CH, stride=S), :] = value[:, e * L : (e + 1) * L]

    @pl.loop(0, CH // 16, unroll=UNROLL)
    def _(g):
        rows = pl.ds(pl.multiple_of(g * 256, 256), 256)
        send[pl.ds(g * 16, 16)] = wide[rows, :].reshape(16, S, L).astype(BF)


def gates(weights, normed, gate):
    @pl.loop(0, S // 2, unroll=UNROLL)
    def _(q):
        gate[q] = sigmoid(
            jnp.dot(weights[4 * CH : 5 * CH, :], normed[q], preferred_element_type=F32)
        )


def gather(recv, mat, turned):
    @pl.loop(0, ROWS, unroll=UNROLL)
    def _(r):
        at = pl.multiple_of(r * 2 * S, 2 * S)
        for p in range(COLS // 2):
            low, high = swap_halves(recv[r * COLS + 2 * p], recv[r * COLS + 2 * p + 1])
            mat[pl.ds(at, S), p * L : (p + 1) * L] = low
            mat[pl.ds(at + S, S), p * L : (p + 1) * L] = high

    if turned is not None:
        for m in range(4):
            for n in range(4):
                turned[n * L : (n + 1) * L, m * L : (m + 1) * L] = mat[
                    m * L : (m + 1) * L, n * L : (n + 1) * L
                ].T


def multiply(torus, lhs, rhs, send, recv, sems):
    for dz in (2, 1, 3, 0):
        plane = torus.planes[dz]
        total = jnp.dot(
            lhs[pl.ds(pl.multiple_of(plane * L, L), L), :], rhs[...], preferred_element_type=F32
        ).astype(BF)
        for k in range(4):
            for p in range(COLS // 2):
                cols = slice(p * L, (p + 1) * L)
                low, high = swap_halves(
                    total[k * 2 * S : k * 2 * S + S, cols],
                    total[k * 2 * S + S : (k + 1) * 2 * S, cols],
                )
                send[plane * 32 + k * COLS + 2 * p] = low
                send[plane * 32 + k * COLS + 2 * p + 1] = high
        for dx, dy, dc in PLANE:
            if (dx, dy, dz, dc) != (0, 0, 0, 0):
                push(torus, torus.at(dx, dy, dz, dc), send, recv, sems)
    recv[torus.me] = send[torus.me]


def shape(recv, wide):
    total = lax.fori_loop(
        0, 8, lambda g, a: a + jnp.sum(recv[pl.ds(g * 16, 16)].astype(F32), axis=0), jnp.zeros((S, L), F32), unroll=UNROLL
    )
    mean = total * (1.0 / CH)

    def squares(g, a):
        center = recv[pl.ds(g * 16, 16)].astype(F32) - mean[None]
        return a + jnp.sum(center * center, axis=0)

    spread = lax.fori_loop(0, 8, squares, jnp.zeros((S, L), F32), unroll=UNROLL) * (1.0 / CH)
    scale = lax.rsqrt(spread + 1e-05)

    @pl.loop(0, 8, unroll=UNROLL)
    def _(g):
        rows = pl.ds(pl.multiple_of(g * 256, 256), 256)
        wide[rows, :] = ((recv[pl.ds(g * 16, 16)].astype(F32) - mean[None]) * scale[None]).reshape(256, L)


def finish(q, wide, weights, gate, base):
    shaped = jnp.concatenate(
        [wide[pl.ds(2 * q + e, CH, stride=S), :] for e in range(2)], axis=1
    ).astype(BF)
    branch = jnp.dot(weights[...], shaped, preferred_element_type=F32)
    return (base[q].astype(F32) + gate[q] * branch).astype(BF)


def kernel(
    pair_hbm, mask_hbm, in1_hbm, gate1_hbm, final1_hbm, in2_hbm, gate2_hbm, final2_hbm, out,
    pair, mask, in1, gate1, final1, in2, gate2, final2, copy_sems,
    base, normed, gate, wide, wide2, wt, ft, keep,
    send_l1, recv_l1, send_r1, recv_r1, send_t1, recv_t1, send_l2, recv_l2, send_r2, recv_r2, send_t2, recv_t2,
    lmat, rmat, turned, send_sems, recv_sems,
):
    torus = Torus()
    row, col = lax.axis_index("row"), lax.axis_index("col")
    sems = [(send_sems.at[k], recv_sems.at[k]) for k in range(6)]
    copies = [
        pltpu.make_async_copy(src, dst, copy_sems.at[k])
        for k, (src, dst) in enumerate(
            ((pair_hbm, pair), (mask_hbm, mask), (in1_hbm, in1), (gate1_hbm, gate1), (final1_hbm, final1),
             (in2_hbm, in2), (gate2_hbm, gate2), (final2_hbm, final2))
        )
    ]
    for copy in copies:
        copy.start()

    barrier = pltpu.get_barrier_semaphore()

    @pl.loop(1, DEVS)
    def _(t):
        pl.semaphore_signal(
            barrier, inc=1, device_id=lax.rem(torus.me + t, DEVS), device_id_type=LOGICAL
        )

    for copy in copies:
        copy.wait()

    for k, (a, b, c) in enumerate(((in1, gate1, final1), (in2, gate2, final2))):
        wt[k, 0 : 4 * CH] = a[...].astype(F32).T.astype(BF)
        wt[k, 4 * CH : 5 * CH] = b[...].astype(F32).T.astype(BF)
        ft[k] = c[...].astype(F32).T.astype(BF)

    held = mask[...].astype(F32)
    spot = lax.broadcasted_iota(jnp.int32, (S, 512), 1)
    line = lax.broadcasted_iota(jnp.int32, (S, 512), 0)
    first = jnp.sum(jnp.where(spot == row * 32 + line, held, 0.0), axis=1, keepdims=True)
    second = jnp.sum(jnp.where(spot == row * 32 + 16 + line, held, 0.0), axis=1, keepdims=True)
    spot = lax.broadcasted_iota(jnp.int32, (L, 512), 1)
    line = lax.broadcasted_iota(jnp.int32, (L, 512), 0)
    across = jnp.sum(
        jnp.where(spot == col * 64 + lax.rem(line, 64), held, 0.0), axis=1, keepdims=True
    )
    across = jnp.broadcast_to(across, (L, L)).T[0:S]
    lane = lax.broadcasted_iota(jnp.int32, (S, L), 1)
    keep[...] = jnp.where(lane < 64, first, second) * across

    @pl.loop(0, S // 2, unroll=UNROLL)
    def _(q):
        values = jnp.concatenate(
            [pair[2 * q], pair[S + 2 * q], pair[2 * q + 1], pair[S + 2 * q + 1]], axis=0
        )
        values = values.astype(F32).T
        base[q] = values.astype(BF)
        normed[q] = norm0(values).astype(BF)

    edge(1, wt.at[0], normed, keep, wide, send_r1)
    pl.semaphore_wait(barrier, DEVS - 1)
    exchange(torus, send_r1, recv_r1, sems[1])
    edge(0, wt.at[0], normed, keep, wide, send_l1)
    exchange(torus, send_l1, recv_l1, sems[0])
    gates(wt.at[0], normed, gate)
    wait_all(recv_r1, sems[1][1])
    gather(recv_r1, rmat, turned)
    wait_all(recv_l1, sems[0][1])
    gather(recv_l1, lmat, None)
    multiply(torus, lmat, turned, send_t1, recv_t1, sems[2])
    wait_all(recv_t1, sems[2][1])
    shape(recv_t1, wide)

    @pl.loop(0, S // 2, unroll=UNROLL)
    def _(q):
        middle = finish(q, wide, ft.at[0], gate, base)
        base[q] = middle
        normed[q] = norm0(middle.astype(F32)).astype(BF)

    edge(0, wt.at[1], normed, keep, wide2, send_l2)
    exchange(torus, send_l2, recv_l2, sems[3])
    edge(1, wt.at[1], normed, keep, wide, send_r2)
    exchange(torus, send_r2, recv_r2, sems[4])
    gates(wt.at[1], normed, gate)
    wait_all(recv_l2, sems[3][1])
    gather(recv_l2, lmat, turned)
    wait_all(recv_r2, sems[4][1])
    gather(recv_r2, rmat, None)
    multiply(torus, turned, rmat, send_t2, recv_t2, sems[5])
    wait_all(recv_t2, sems[5][1])
    shape(recv_t2, wide)

    @pl.loop(0, S // 2, unroll=UNROLL)
    def _(q):
        done = finish(q, wide, ft.at[1], gate, base).astype(F32).T.astype(BF)
        out[2 * q] = done[0:64]
        out[S + 2 * q] = done[64:128]
        out[2 * q + 1] = done[128:192]
        out[S + 2 * q + 1] = done[192:256]

    for k, ref in enumerate((send_l1, send_r1, send_t1, send_l2, send_r2, send_t2)):
        wait_all(ref, sems[k][0])


def shards(*args):
    pair, mask, *weights = args
    operands = (pair, mask.reshape(1, 512), *weights)
    tiles = pltpu.VMEM((DEVS, S, L), BF)
    square = pltpu.VMEM((512, 512), BF)
    return pl.pallas_call(
        kernel,
        out_shape=jax.ShapeDtypeStruct(pair.shape, BF),
        in_specs=[pl.BlockSpec(memory_space=pltpu.HBM)] * 8,
        out_specs=pl.BlockSpec(memory_space=pltpu.VMEM),
        scratch_shapes=[
            *[pltpu.VMEM(v.shape, v.dtype) for v in operands],
            pltpu.SemaphoreType.DMA((8,)),
            pltpu.VMEM((S // 2, CH, 2 * L), BF),
            pltpu.VMEM((S // 2, CH, 2 * L), BF),
            pltpu.VMEM((S // 2, CH, 2 * L), F32),
            pltpu.VMEM((CH * S, L), F32),
            pltpu.VMEM((CH * S, L), F32),
            pltpu.VMEM((2, 5 * CH, CH), BF),
            pltpu.VMEM((2, CH, CH), BF),
            pltpu.VMEM((S, L), F32),
            *[tiles] * 12,
            square, square, square,
            pltpu.SemaphoreType.DMA((6,)),
            pltpu.SemaphoreType.DMA((6,)),
        ],
        compiler_params=pltpu.CompilerParams(
            collective_id=0, has_side_effects=True, vmem_limit_bytes=VMEM_BYTES
        ),
    )(*operands)


def solution(mesh):
    return jax.shard_map(
        shards,
        mesh=mesh,
        in_specs=(P("row", "col", None), P(), P(), P(), P(), P(), P(), P()),
        out_specs=P("row", "col", None),
        check_vma=False,
    )
```

```python
import jax
import jax.numpy as jnp
from jax import lax
from jax.experimental import pallas as pl
from jax.experimental.pallas import tpu as pltpu
from jax.sharding import PartitionSpec as P

VMEM_BYTES = 32 * 2**20
UNROLL = True
LOGICAL = pl.DeviceIdType.LOGICAL
CH = 128
S = 16
L = 128
DEVS = 128
ROWS = 16
COLS = 8
BF = jnp.bfloat16
F32 = jnp.float32
ORDER = sorted(
    ((dx, dy, dz, dc) for dz in range(4) for dy in range(4) for dx in range(4) for dc in range(2)),
    key=lambda o: -sum(min(v, 4 - v) for v in o[:3]),
)
ORDER.remove((0, 0, 0, 0))


def half(axis, odd):
    return [o for o in ORDER if o[axis] % 2 == odd]


class Torus:
    def __init__(self):
        row, col = lax.axis_index("row"), lax.axis_index("col")
        self.me = row * COLS + col
        self.z = row // 4
        y = lax.rem(col, 2) * 2 + lax.rem(row // 2, 2)
        self.planes = [lax.rem(self.z + d, 4) for d in range(4)]
        ys = [lax.rem(y + d, 4) for d in range(4)]
        self.ys = [lax.rem(v, 2) * 16 + v // 2 for v in ys]
        self.xs = [lax.rem(col // 2 + d, 4) * 2 for d in range(4)]
        self.cs = [lax.rem(lax.rem(row, 2) + d, 2) * 8 for d in range(2)]

    def at(self, dx, dy, dz, dc):
        return self.planes[dz] * 32 + self.ys[dy] + self.xs[dx] + self.cs[dc]


def sigmoid(v):
    return 0.5 * jnp.tanh(0.5 * v) + 0.5


def norm0(v):
    center = v - jnp.mean(v, axis=0, keepdims=True)
    spread = jnp.mean(center * center, axis=0, keepdims=True)
    return center * lax.rsqrt(spread + 1e-05)


def swap_halves(first, second):
    low = lax.broadcasted_iota(jnp.int32, first.shape, 1) < 64
    return (
        jnp.where(low, first, pltpu.roll(second, 64, 1)),
        jnp.where(low, pltpu.roll(first, 64, 1), second),
    )


def push(torus, to, send, recv, sems):
    pltpu.make_async_remote_copy(
        src_ref=send.at[to],
        dst_ref=recv.at[torus.me],
        send_sem=sems[0],
        recv_sem=sems[1],
        device_id=to,
        device_id_type=LOGICAL,
    ).start()


def exchange(torus, offsets, send, recv, sems):
    for offset in offsets:
        push(torus, torus.at(*offset), send, recv, sems)


def wait_for(ref, count, sem):
    some = ref.at[pl.ds(0, count)]
    pltpu.make_async_copy(some, some, sem).wait()


def edge(side, weights, normed, keep, wide, send):
    @pl.loop(0, S // 2, unroll=UNROLL)
    def _(q):
        proj = jnp.dot(
            weights[side * 2 * CH : (side + 1) * 2 * CH, :], normed[q], preferred_element_type=F32
        )
        mask = jnp.concatenate([keep[pl.ds(2 * q, 1), :], keep[pl.ds(2 * q + 1, 1), :]], axis=1)
        value = mask * sigmoid(proj[0:CH]) * proj[CH : 2 * CH]
        for e in range(2):
            wide[pl.ds(2 * q + e, CH, stride=S), :] = value[:, e * L : (e + 1) * L]

    @pl.loop(0, CH // 16, unroll=UNROLL)
    def _(g):
        rows = pl.ds(pl.multiple_of(g * 256, 256), 256)
        send[pl.ds(g * 16, 16)] = wide[rows, :].reshape(16, S, L).astype(BF)


def gates(weights, normed, gate):
    @pl.loop(0, S // 2, unroll=UNROLL)
    def _(q):
        gate[q] = sigmoid(
            jnp.dot(weights[4 * CH : 5 * CH, :], normed[q], preferred_element_type=F32)
        )


def gather(recv, mat):
    for r in range(ROWS):
        for p in range(COLS // 2):
            low, high = swap_halves(recv[r * COLS + 2 * p], recv[r * COLS + 2 * p + 1])
            mat[r * 2 * S : r * 2 * S + S, p * L : (p + 1) * L] = low
            mat[r * 2 * S + S : (r + 1) * 2 * S, p * L : (p + 1) * L] = high


def turn(mat, turned):
    for m in range(4):
        for n in range(4):
            turned[n * L : (n + 1) * L, m * L : (m + 1) * L] = mat[
                m * L : (m + 1) * L, n * L : (n + 1) * L
            ].T


def outgoing(torus, odd, recv_l, lhs, rhs, send):
    planes = [torus.planes[odd], torus.planes[odd + 2]]
    for n, plane in enumerate(planes):
        for k in range(4):
            for p in range(COLS // 2):
                at = plane * 32 + k * COLS + 2 * p
                low, high = swap_halves(recv_l[at], recv_l[at + 1])
                row = n * L + k * 2 * S
                lhs[row : row + S, p * L : (p + 1) * L] = low
                lhs[row + S : row + 2 * S, p * L : (p + 1) * L] = high
    total = jnp.dot(lhs[...], rhs[...], preferred_element_type=F32).astype(BF)
    for n, plane in enumerate(planes):
        for k in range(4):
            row = n * L + k * 2 * S
            for p in range(COLS // 2):
                cols = slice(p * L, (p + 1) * L)
                low, high = swap_halves(total[row : row + S, cols], total[row + S : row + 2 * S, cols])
                at = plane * 32 + k * COLS + 2 * p
                send[at] = low
                send[at + 1] = high


def incoming(torus, odd, recv_r, lhs, rhs, send):
    for r in range(ROWS):
        for n in range(2):
            at = r * COLS + torus.xs[odd + 2 * n]
            low, high = swap_halves(recv_r[at], recv_r[at + 1])
            rhs[r * 2 * S : r * 2 * S + S, n * L : (n + 1) * L] = low
            rhs[r * 2 * S + S : (r + 1) * 2 * S, n * L : (n + 1) * L] = high
    for m in range(2):
        total = jnp.dot(lhs[m * 256 : (m + 1) * 256, :], rhs[...], preferred_element_type=F32).astype(BF)
        for k in range(8):
            for n in range(2):
                cols = slice(n * L, (n + 1) * L)
                low, high = swap_halves(
                    total[k * 2 * S : k * 2 * S + S, cols], total[k * 2 * S + S : (k + 1) * 2 * S, cols]
                )
                at = (m * 8 + k) * COLS + torus.xs[odd + 2 * n]
                send[at] = low
                send[at + 1] = high


def shape(recv, wide):
    total = lax.fori_loop(
        0, 8, lambda g, a: a + jnp.sum(recv[pl.ds(g * 16, 16)].astype(F32), axis=0), jnp.zeros((S, L), F32), unroll=UNROLL
    )
    mean = total * (1.0 / CH)

    def squares(g, a):
        center = recv[pl.ds(g * 16, 16)].astype(F32) - mean[None]
        return a + jnp.sum(center * center, axis=0)

    spread = lax.fori_loop(0, 8, squares, jnp.zeros((S, L), F32), unroll=UNROLL) * (1.0 / CH)
    scale = lax.rsqrt(spread + 1e-05)

    @pl.loop(0, 8, unroll=UNROLL)
    def _(g):
        rows = pl.ds(pl.multiple_of(g * 256, 256), 256)
        wide[rows, :] = ((recv[pl.ds(g * 16, 16)].astype(F32) - mean[None]) * scale[None]).reshape(256, L)


def finish(q, wide, weights, gate, base):
    shaped = jnp.concatenate(
        [wide[pl.ds(2 * q + e, CH, stride=S), :] for e in range(2)], axis=1
    ).astype(BF)
    branch = jnp.dot(weights[...], shaped, preferred_element_type=F32)
    return (base[q].astype(F32) + gate[q] * branch).astype(BF)


def kernel(
    pair_hbm, mask_hbm, in1_hbm, gate1_hbm, final1_hbm, in2_hbm, gate2_hbm, final2_hbm, out,
    pair, mask, in1, gate1, final1, in2, gate2, final2, copy_sems,
    base, normed, gate, wide, wide2, wt, ft, keep,
    send_l1, recv_l1, send_r1, recv_r1, send_t1, recv_t1, send_l2, recv_l2, send_r2, recv_r2, send_t2, recv_t2,
    mat, turned, part_a, part_b, send_sems, recv_sems,
):
    torus = Torus()
    row, col = lax.axis_index("row"), lax.axis_index("col")
    copies = [
        pltpu.make_async_copy(src, dst, copy_sems.at[k])
        for k, (src, dst) in enumerate(
            ((pair_hbm, pair), (mask_hbm, mask), (in1_hbm, in1), (gate1_hbm, gate1), (final1_hbm, final1),
             (in2_hbm, in2), (gate2_hbm, gate2), (final2_hbm, final2))
        )
    ]
    for copy in copies:
        copy.start()

    barrier = pltpu.get_barrier_semaphore()

    @pl.loop(1, DEVS)
    def _(t):
        pl.semaphore_signal(
            barrier, inc=1, device_id=lax.rem(torus.me + t, DEVS), device_id_type=LOGICAL
        )

    for copy in copies:
        copy.wait()

    wt[0, 2 * CH : 4 * CH] = in1[:, 2 * CH : 4 * CH].T

    held = mask[...].astype(F32)
    spot = lax.broadcasted_iota(jnp.int32, (S, 512), 1)
    line = lax.broadcasted_iota(jnp.int32, (S, 512), 0)
    first = jnp.sum(jnp.where(spot == row * 32 + line, held, 0.0), axis=1, keepdims=True)
    second = jnp.sum(jnp.where(spot == row * 32 + 16 + line, held, 0.0), axis=1, keepdims=True)
    spot = lax.broadcasted_iota(jnp.int32, (L, 512), 1)
    line = lax.broadcasted_iota(jnp.int32, (L, 512), 0)
    across = jnp.sum(
        jnp.where(spot == col * 64 + lax.rem(line, 64), held, 0.0), axis=1, keepdims=True
    )
    across = jnp.broadcast_to(across, (L, L)).T[0:S]
    lane = lax.broadcasted_iota(jnp.int32, (S, L), 1)
    keep[...] = jnp.where(lane < 64, first, second) * across

    @pl.loop(0, S // 2, unroll=UNROLL)
    def _(q):
        values = jnp.concatenate(
            [pair[2 * q], pair[S + 2 * q], pair[2 * q + 1], pair[S + 2 * q + 1]], axis=0
        )
        values = values.astype(F32).T
        base[q] = values.astype(BF)
        normed[q] = norm0(values).astype(BF)

    edge(1, wt.at[0], normed, keep, wide, send_r1)
    pl.semaphore_wait(barrier, DEVS - 1)
    sems = [(send_sems.at[k], recv_sems.at[k]) for k in range(10)]
    exchange(torus, ORDER, send_r1, recv_r1, sems[0])
    wt[0, 0 : 2 * CH] = in1[:, 0 : 2 * CH].T
    edge(0, wt.at[0], normed, keep, wide, send_l1)
    for odd in range(2):
        exchange(torus, half(2, odd), send_l1, recv_l1, sems[1 + odd])
    recv_r1[torus.me] = send_r1[torus.me]
    recv_l1[torus.me] = send_l1[torus.me]

    wt[0, 4 * CH : 5 * CH] = gate1[...].T
    wt[1, 0 : 4 * CH] = in2[...].T
    wt[1, 4 * CH : 5 * CH] = gate2[...].T
    ft[0] = final1[...].T
    ft[1] = final2[...].T
    gates(wt.at[0], normed, gate)

    wait_for(recv_r1, DEVS - 1, sems[0][1])
    gather(recv_r1, mat)
    turn(mat, turned)
    for odd in range(2):
        wait_for(recv_l1, len(half(2, odd)), sems[1 + odd][1])
        outgoing(torus, odd, recv_l1, (part_a, part_b)[odd], turned, send_t1)
        exchange(torus, half(2, odd), send_t1, recv_t1, sems[3 + odd])
    recv_t1[torus.me] = send_t1[torus.me]
    for odd in range(2):
        wait_for(recv_t1, len(half(2, odd)), sems[3 + odd][1])
    shape(recv_t1, wide)

    @pl.loop(0, S // 2, unroll=UNROLL)
    def _(q):
        middle = finish(q, wide, ft.at[0], gate, base)
        base[q] = middle
        normed[q] = norm0(middle.astype(F32)).astype(BF)

    edge(0, wt.at[1], normed, keep, wide2, send_l2)
    exchange(torus, ORDER, send_l2, recv_l2, sems[5])
    edge(1, wt.at[1], normed, keep, wide, send_r2)
    for odd in range(2):
        exchange(torus, half(0, odd), send_r2, recv_r2, sems[6 + odd])
    recv_l2[torus.me] = send_l2[torus.me]
    recv_r2[torus.me] = send_r2[torus.me]

    gates(wt.at[1], normed, gate)

    wait_for(recv_l2, DEVS - 1, sems[5][1])
    gather(recv_l2, mat)
    turn(mat, turned)
    for odd in range(2):
        wait_for(recv_r2, len(half(0, odd)), sems[6 + odd][1])
        incoming(torus, odd, recv_r2, turned, (mat.at[:, 0:256], mat.at[:, 256:512])[odd], send_t2)
        exchange(torus, half(0, odd), send_t2, recv_t2, sems[8 + odd])
    recv_t2[torus.me] = send_t2[torus.me]
    for odd in range(2):
        wait_for(recv_t2, len(half(0, odd)), sems[8 + odd][1])
    shape(recv_t2, wide)

    @pl.loop(0, S // 2, unroll=UNROLL)
    def _(q):
        done = finish(q, wide, ft.at[1], gate, base).astype(F32).T.astype(BF)
        out[2 * q] = done[0:64]
        out[S + 2 * q] = done[64:128]
        out[2 * q + 1] = done[128:192]
        out[S + 2 * q + 1] = done[192:256]

    for k, ref in ((0, send_r1), (5, send_l2)):
        wait_for(ref, DEVS - 1, sems[k][0])
    for k, ref in ((1, send_l1), (3, send_t1), (6, send_r2), (8, send_t2)):
        for odd in range(2):
            wait_for(ref, len(half(0, odd)), sems[k + odd][0])


def shards(*args):
    pair, mask, *weights = args
    operands = (pair, mask.reshape(1, 512), *weights)
    operands = [pltpu.with_memory_space_constraint(v, pltpu.HBM) for v in operands]
    tiles = pltpu.VMEM((DEVS, S, L), BF)
    square = pltpu.VMEM((512, 512), BF)
    return pl.pallas_call(
        kernel,
        out_shape=pltpu.VMEM(pair.shape, BF),
        in_specs=[pl.BlockSpec(memory_space=pltpu.HBM)] * 8,
        out_specs=pl.BlockSpec(memory_space=pltpu.VMEM),
        scratch_shapes=[
            *[pltpu.VMEM(v.shape, v.dtype) for v in operands],
            pltpu.SemaphoreType.DMA((8,)),
            pltpu.VMEM((S // 2, CH, 2 * L), BF),
            pltpu.VMEM((S // 2, CH, 2 * L), BF),
            pltpu.VMEM((S // 2, CH, 2 * L), F32),
            pltpu.VMEM((CH * S, L), F32),
            pltpu.VMEM((CH * S, L), F32),
            pltpu.VMEM((2, 5 * CH, CH), BF),
            pltpu.VMEM((2, CH, CH), BF),
            pltpu.VMEM((S, L), F32),
            *[tiles] * 12,
            square, square,
            pltpu.VMEM((256, 512), BF),
            pltpu.VMEM((256, 512), BF),
            pltpu.SemaphoreType.DMA((10,)),
            pltpu.SemaphoreType.DMA((10,)),
        ],
        compiler_params=pltpu.CompilerParams(
            collective_id=0, has_side_effects=True, vmem_limit_bytes=VMEM_BYTES
        ),
    )(*operands)


def solution(mesh):
    return jax.shard_map(
        shards,
        mesh=mesh,
        in_specs=(P("row", "col", None), P(), P(), P(), P(), P(), P(), P()),
        out_specs=P("row", "col", None),
        check_vma=False,
    )
```

```python
import jax
import jax.numpy as jnp
from jax import lax
from jax.experimental import pallas as pl
from jax.experimental.pallas import tpu as pltpu
from jax.sharding import PartitionSpec as P

VMEM_BYTES = 32 * 2**20
UNROLL = True
LOGICAL = pl.DeviceIdType.LOGICAL
CH = 128
S = 16
L = 128
DEVS = 128
ROWS = 16
COLS = 8
BF = jnp.bfloat16
F32 = jnp.float32
ORDER = sorted(
    ((dx, dy, dz, dc) for dz in range(4) for dy in range(4) for dx in range(4) for dc in range(2)),
    key=lambda o: -sum(min(v, 4 - v) for v in o[:3]),
)
ORDER.remove((0, 0, 0, 0))


def half(axis, odd):
    return [o for o in ORDER if o[axis] % 2 == odd]


class Torus:
    def __init__(self):
        row, col = lax.axis_index("row"), lax.axis_index("col")
        self.me = row * COLS + col
        self.z = row // 4
        y = lax.rem(col, 2) * 2 + lax.rem(row // 2, 2)
        self.planes = [lax.rem(self.z + d, 4) for d in range(4)]
        ys = [lax.rem(y + d, 4) for d in range(4)]
        self.ys = [lax.rem(v, 2) * 16 + v // 2 for v in ys]
        self.xs = [lax.rem(col // 2 + d, 4) * 2 for d in range(4)]
        self.cs = [lax.rem(lax.rem(row, 2) + d, 2) * 8 for d in range(2)]

    def at(self, dx, dy, dz, dc):
        return self.planes[dz] * 32 + self.ys[dy] + self.xs[dx] + self.cs[dc]


def turn_half(weights):
    return (weights.astype(F32) * 0.5).astype(BF).T


def norm0(v):
    center = v - jnp.mean(v, axis=0, keepdims=True)
    spread = jnp.mean(center * center, axis=0, keepdims=True)
    return center * lax.rsqrt(spread + 1e-05)


def swap_halves(first, second):
    low = lax.broadcasted_iota(jnp.int32, first.shape, 1) < 64
    return (
        jnp.where(low, first, pltpu.roll(second, 64, 1)),
        jnp.where(low, pltpu.roll(first, 64, 1), second),
    )


def push(torus, to, send, recv, sems):
    pltpu.make_async_remote_copy(
        src_ref=send.at[to],
        dst_ref=recv.at[torus.me],
        send_sem=sems[0],
        recv_sem=sems[1],
        device_id=to,
        device_id_type=LOGICAL,
    ).start()


def exchange(torus, offsets, send, recv, sems):
    for offset in offsets:
        push(torus, torus.at(*offset), send, recv, sems)


def wait_for(ref, count, sem):
    some = ref.at[pl.ds(0, count)]
    pltpu.make_async_copy(some, some, sem).wait()


def edge(side, weights, normed, keep, wide, send):
    @pl.loop(0, S // 2, unroll=UNROLL)
    def _(q):
        proj = jnp.dot(
            weights[side * 2 * CH : (side + 1) * 2 * CH, :], normed[q], preferred_element_type=F32
        )
        mask = jnp.concatenate([keep[pl.ds(2 * q, 1), :], keep[pl.ds(2 * q + 1, 1), :]], axis=1)
        value = mask * (jnp.tanh(proj[0:CH]) + 1.0) * proj[CH : 2 * CH]
        for e in range(2):
            wide[pl.ds(2 * q + e, CH, stride=S), :] = value[:, e * L : (e + 1) * L]

    @pl.loop(0, CH // 16, unroll=UNROLL)
    def _(g):
        rows = pl.ds(pl.multiple_of(g * 256, 256), 256)
        send[pl.ds(g * 16, 16)] = wide[rows, :].reshape(16, S, L).astype(BF)


def gates(weights, normed, gate):
    @pl.loop(0, S // 2, unroll=UNROLL)
    def _(q):
        proj = jnp.dot(weights[4 * CH : 5 * CH, :], normed[q], preferred_element_type=F32)
        gate[q] = jnp.tanh(proj) + 1.0


def gather(recv, mat):
    for r in range(ROWS):
        for p in range(COLS // 2):
            low, high = swap_halves(recv[r * COLS + 2 * p], recv[r * COLS + 2 * p + 1])
            mat[r * 2 * S : r * 2 * S + S, p * L : (p + 1) * L] = low
            mat[r * 2 * S + S : (r + 1) * 2 * S, p * L : (p + 1) * L] = high


def turn(mat, turned):
    for m in range(4):
        for n in range(4):
            turned[n * L : (n + 1) * L, m * L : (m + 1) * L] = mat[
                m * L : (m + 1) * L, n * L : (n + 1) * L
            ].T


def outgoing(torus, odd, recv_l, lhs, rhs, send):
    planes = [torus.planes[odd], torus.planes[odd + 2]]
    for n, plane in enumerate(planes):
        for k in range(4):
            for p in range(COLS // 2):
                at = plane * 32 + k * COLS + 2 * p
                low, high = swap_halves(recv_l[at], recv_l[at + 1])
                row = n * L + k * 2 * S
                lhs[row : row + S, p * L : (p + 1) * L] = low
                lhs[row + S : row + 2 * S, p * L : (p + 1) * L] = high
    total = jnp.dot(lhs[...], rhs[...], preferred_element_type=F32).astype(BF)
    for n, plane in enumerate(planes):
        for k in range(4):
            row = n * L + k * 2 * S
            for p in range(COLS // 2):
                cols = slice(p * L, (p + 1) * L)
                low, high = swap_halves(total[row : row + S, cols], total[row + S : row + 2 * S, cols])
                at = plane * 32 + k * COLS + 2 * p
                send[at] = low
                send[at + 1] = high


def incoming(torus, odd, recv_r, lhs, rhs, send):
    for r in range(ROWS):
        for n in range(2):
            at = r * COLS + torus.xs[odd + 2 * n]
            low, high = swap_halves(recv_r[at], recv_r[at + 1])
            rhs[r * 2 * S : r * 2 * S + S, n * L : (n + 1) * L] = low
            rhs[r * 2 * S + S : (r + 1) * 2 * S, n * L : (n + 1) * L] = high
    for m in range(2):
        total = jnp.dot(lhs[m * 256 : (m + 1) * 256, :], rhs[...], preferred_element_type=F32).astype(BF)
        for k in range(8):
            for n in range(2):
                cols = slice(n * L, (n + 1) * L)
                low, high = swap_halves(
                    total[k * 2 * S : k * 2 * S + S, cols], total[k * 2 * S + S : (k + 1) * 2 * S, cols]
                )
                at = (m * 8 + k) * COLS + torus.xs[odd + 2 * n]
                send[at] = low
                send[at + 1] = high


def spread(recv, starts, count, wide, shift):
    total = jnp.zeros((S, L), F32)
    square = jnp.zeros((S, L), F32)
    for at in starts:
        tiles = recv[pl.ds(at, count)].astype(F32)
        wide[pl.ds(pl.multiple_of(at * S, count * S), count * S), :] = tiles.reshape(count * S, L)
        if shift is not None:
            tiles = tiles - shift[None]
            square = square + jnp.sum(tiles * tiles, axis=0)
        total = total + jnp.sum(tiles, axis=0)
    mean = total * (2.0 / CH)
    if shift is None:
        for at in starts:
            tiles = recv[pl.ds(at, count)].astype(F32) - mean[None]
            square = square + jnp.sum(tiles * tiles, axis=0)
    return mean, square


def z_starts(torus, odd):
    return [torus.planes[odd + 2 * n] * 32 + k * 16 for n in range(2) for k in range(2)]


def x_starts(torus, odd):
    return [r * COLS + torus.xs[odd + 2 * n] for r in range(ROWS) for n in range(2)]


def statistics(torus, axis, recv, sems, wide, stats):
    starts, count = (z_starts, 16) if axis == 2 else (x_starts, 2)
    wait_for(recv, len(half(axis, 0)), sems[0][1])
    mean, square = spread(recv, starts(torus, 0), count, wide, None)
    wait_for(recv, len(half(axis, 1)), sems[1][1])
    apart, more = spread(recv, starts(torus, 1), count, wide, mean)
    spread_all = (square + more - (CH / 4.0) * apart * apart) * (1.0 / CH)
    stats[0] = mean + 0.5 * apart
    stats[1] = lax.rsqrt(spread_all + 1e-05)


def finish(q, wide, stats, weights, gate, base):
    shaped = []
    for s in (2 * q, 2 * q + 1):
        row = pl.ds(s, 1)
        shaped.append((wide[pl.ds(s, CH, stride=S), :] - stats[0, row, :]) * stats[1, row, :])
    shaped = jnp.concatenate(shaped, axis=1).astype(BF)
    branch = jnp.dot(weights[...], shaped, preferred_element_type=F32)
    return (base[q].astype(F32) + gate[q] * branch).astype(BF)


def kernel(
    pair_hbm, mask_hbm, in1_hbm, gate1_hbm, final1_hbm, in2_hbm, gate2_hbm, final2_hbm, out,
    pair, mask, in1, gate1, final1, in2, gate2, final2, copy_sems,
    base, normed, gate, wide, wide2, wt, ft, keep, stats,
    send_l1, recv_l1, send_r1, recv_r1, send_t1, recv_t1, send_l2, recv_l2, send_r2, recv_r2, send_t2, recv_t2,
    mat, turned, part_a, part_b, send_sems, recv_sems,
):
    torus = Torus()
    row, col = lax.axis_index("row"), lax.axis_index("col")
    copies = [
        pltpu.make_async_copy(src, dst, copy_sems.at[k])
        for k, (src, dst) in enumerate(
            ((pair_hbm, pair), (mask_hbm, mask), (in1_hbm, in1), (gate1_hbm, gate1), (final1_hbm, final1),
             (in2_hbm, in2), (gate2_hbm, gate2), (final2_hbm, final2))
        )
    ]
    for copy in copies:
        copy.start()

    barrier = pltpu.get_barrier_semaphore()

    @pl.loop(1, DEVS)
    def _(t):
        pl.semaphore_signal(
            barrier, inc=1, device_id=lax.rem(torus.me + t, DEVS), device_id_type=LOGICAL
        )

    for copy in copies:
        copy.wait()

    wt[0, 2 * CH : 4 * CH] = turn_half(in1[:, 2 * CH : 4 * CH])

    held = mask[...].astype(F32)
    spot = lax.broadcasted_iota(jnp.int32, (S, 512), 1)
    line = lax.broadcasted_iota(jnp.int32, (S, 512), 0)
    first = jnp.sum(jnp.where(spot == row * 32 + line, held, 0.0), axis=1, keepdims=True)
    second = jnp.sum(jnp.where(spot == row * 32 + 16 + line, held, 0.0), axis=1, keepdims=True)
    spot = lax.broadcasted_iota(jnp.int32, (L, 512), 1)
    line = lax.broadcasted_iota(jnp.int32, (L, 512), 0)
    across = jnp.sum(
        jnp.where(spot == col * 64 + lax.rem(line, 64), held, 0.0), axis=1, keepdims=True
    )
    across = jnp.broadcast_to(across, (L, L)).T[0:S]
    lane = lax.broadcasted_iota(jnp.int32, (S, L), 1)
    keep[...] = jnp.where(lane < 64, first, second) * across

    @pl.loop(0, S // 2, unroll=UNROLL)
    def _(q):
        values = jnp.concatenate(
            [pair[2 * q], pair[S + 2 * q], pair[2 * q + 1], pair[S + 2 * q + 1]], axis=0
        )
        values = values.T
        base[q] = values
        normed[q] = norm0(values.astype(F32)).astype(BF)

    edge(1, wt.at[0], normed, keep, wide, send_r1)
    pl.semaphore_wait(barrier, DEVS - 1)
    sems = [(send_sems.at[k], recv_sems.at[k]) for k in range(10)]
    exchange(torus, ORDER, send_r1, recv_r1, sems[0])
    wt[0, 0 : 2 * CH] = turn_half(in1[:, 0 : 2 * CH])
    edge(0, wt.at[0], normed, keep, wide, send_l1)
    for odd in range(2):
        exchange(torus, half(2, odd), send_l1, recv_l1, sems[1 + odd])
    recv_r1[torus.me] = send_r1[torus.me]
    recv_l1[torus.me] = send_l1[torus.me]

    wt[0, 4 * CH : 5 * CH] = turn_half(gate1[...])
    wt[1, 0 : 4 * CH] = turn_half(in2[...])
    wt[1, 4 * CH : 5 * CH] = turn_half(gate2[...])
    ft[0] = turn_half(final1[...])
    ft[1] = turn_half(final2[...])
    gates(wt.at[0], normed, gate)

    wait_for(recv_r1, DEVS - 1, sems[0][1])
    gather(recv_r1, mat)
    turn(mat, turned)
    for odd in range(2):
        wait_for(recv_l1, len(half(2, odd)), sems[1 + odd][1])
        outgoing(torus, odd, recv_l1, (part_a, part_b)[odd], turned, send_t1)
        exchange(torus, half(2, odd), send_t1, recv_t1, sems[3 + odd])
    recv_t1[torus.me] = send_t1[torus.me]
    statistics(torus, 2, recv_t1, sems[3:5], wide, stats)

    @pl.loop(0, S // 2, unroll=UNROLL)
    def _(q):
        middle = finish(q, wide, stats, ft.at[0], gate, base)
        base[q] = middle
        normed[q] = norm0(middle.astype(F32)).astype(BF)

    edge(0, wt.at[1], normed, keep, wide2, send_l2)
    exchange(torus, ORDER, send_l2, recv_l2, sems[5])
    edge(1, wt.at[1], normed, keep, wide, send_r2)
    for odd in range(2):
        exchange(torus, half(0, odd), send_r2, recv_r2, sems[6 + odd])
    recv_l2[torus.me] = send_l2[torus.me]
    recv_r2[torus.me] = send_r2[torus.me]

    gates(wt.at[1], normed, gate)

    wait_for(recv_l2, DEVS - 1, sems[5][1])
    gather(recv_l2, mat)
    turn(mat, turned)
    for odd in range(2):
        wait_for(recv_r2, len(half(0, odd)), sems[6 + odd][1])
        incoming(torus, odd, recv_r2, turned, (mat.at[:, 0:256], mat.at[:, 256:512])[odd], send_t2)
        exchange(torus, half(0, odd), send_t2, recv_t2, sems[8 + odd])
    recv_t2[torus.me] = send_t2[torus.me]
    statistics(torus, 0, recv_t2, sems[8:10], wide, stats)

    @pl.loop(0, S // 2, unroll=UNROLL)
    def _(q):
        done = finish(q, wide, stats, ft.at[1], gate, base).T
        out[2 * q] = done[0:64]
        out[S + 2 * q] = done[64:128]
        out[2 * q + 1] = done[128:192]
        out[S + 2 * q + 1] = done[192:256]

    for k, ref in ((0, send_r1), (5, send_l2)):
        wait_for(ref, DEVS - 1, sems[k][0])
    for k, ref in ((1, send_l1), (3, send_t1), (6, send_r2), (8, send_t2)):
        for odd in range(2):
            wait_for(ref, len(half(0, odd)), sems[k + odd][0])


def shards(*args):
    pair, mask, *weights = args
    operands = (pair, mask.reshape(1, 512), *weights)
    operands = [pltpu.with_memory_space_constraint(v, pltpu.HBM) for v in operands]
    tiles = pltpu.VMEM((DEVS, S, L), BF)
    square = pltpu.VMEM((512, 512), BF)
    return pl.pallas_call(
        kernel,
        out_shape=pltpu.VMEM(pair.shape, BF),
        in_specs=[pl.BlockSpec(memory_space=pltpu.HBM)] * 8,
        out_specs=pl.BlockSpec(memory_space=pltpu.VMEM),
        scratch_shapes=[
            *[pltpu.VMEM(v.shape, v.dtype) for v in operands],
            pltpu.SemaphoreType.DMA((8,)),
            pltpu.VMEM((S // 2, CH, 2 * L), BF),
            pltpu.VMEM((S // 2, CH, 2 * L), BF),
            pltpu.VMEM((S // 2, CH, 2 * L), F32),
            pltpu.VMEM((CH * S, L), F32),
            pltpu.VMEM((CH * S, L), F32),
            pltpu.VMEM((2, 5 * CH, CH), BF),
            pltpu.VMEM((2, CH, CH), BF),
            pltpu.VMEM((S, L), F32),
            pltpu.VMEM((2, S, L), F32),
            *[tiles] * 12,
            square, square,
            pltpu.VMEM((256, 512), BF),
            pltpu.VMEM((256, 512), BF),
            pltpu.SemaphoreType.DMA((10,)),
            pltpu.SemaphoreType.DMA((10,)),
        ],
        compiler_params=pltpu.CompilerParams(
            collective_id=0, has_side_effects=True, vmem_limit_bytes=VMEM_BYTES
        ),
    )(*operands)


def solution(mesh):
    return jax.shard_map(
        shards,
        mesh=mesh,
        in_specs=(P("row", "col", None), P(), P(), P(), P(), P(), P(), P()),
        out_specs=P("row", "col", None),
        check_vma=False,
    )
```

```python
import jax
import jax.numpy as jnp
from jax import lax
from jax.experimental import pallas as pl
from jax.experimental.pallas import tpu as pltpu
from jax.sharding import PartitionSpec as P

VMEM_BYTES = 32 * 2**20
UNROLL = True
LOGICAL = pl.DeviceIdType.LOGICAL
CH = 128
S = 16
L = 128
DEVS = 128
ROWS = 16
COLS = 8
BF = jnp.bfloat16
F32 = jnp.float32
ORDER = sorted(
    ((dx, dy, dz, dc) for dz in range(4) for dy in range(4) for dx in range(4) for dc in range(2)),
    key=lambda o: -sum(min(v, 4 - v) for v in o[:3]),
)
ORDER.remove((0, 0, 0, 0))


def half(axis, odd):
    return [o for o in ORDER if o[axis] % 2 == odd]


class Torus:
    def __init__(self):
        row, col = lax.axis_index("row"), lax.axis_index("col")
        self.me = row * COLS + col
        self.z = row // 4
        y = lax.rem(col, 2) * 2 + lax.rem(row // 2, 2)
        self.planes = [lax.rem(self.z + d, 4) for d in range(4)]
        columns = [lax.rem(col // 2 + d, 4) for d in range(4)]
        ys = [lax.rem(y + d, 4) for d in range(4)]
        self.ys = [lax.rem(v, 2) * 16 + v // 2 for v in ys]
        self.xs = [v * 2 for v in columns]
        self.cs = [lax.rem(lax.rem(row, 2) + d, 2) * 8 for d in range(2)]

        self.late = ([jnp.minimum(v, 2) for v in columns], [jnp.minimum(v, 2) for v in ys], self.planes)

    def at(self, dx, dy, dz, dc):
        return self.planes[dz] * 32 + self.ys[dy] + self.xs[dx] + self.cs[dc]


def turn_half(weights):
    return (weights.astype(F32) * 0.5).astype(BF).T


def norm0(v):
    center = v - jnp.mean(v, axis=0, keepdims=True)
    spread = jnp.mean(center * center, axis=0, keepdims=True)
    return center * lax.rsqrt(spread + 1e-05)


def swap_halves(first, second):
    low = lax.broadcasted_iota(jnp.int32, first.shape, 1) < 64
    return (
        jnp.where(low, first, pltpu.roll(second, 64, 1)),
        jnp.where(low, pltpu.roll(first, 64, 1), second),
    )


def push(torus, to, send, recv, sems):
    pltpu.make_async_remote_copy(
        src_ref=send.at[to],
        dst_ref=recv.at[torus.me],
        send_sem=sems[0],
        recv_sem=sems[1],
        device_id=to,
        device_id_type=LOGICAL,
    ).start()


def exchange(torus, offsets, send, recv, sems):
    for offset in offsets:
        push(torus, torus.at(*offset), send, recv, sems)


def exchange_some(torus, offsets, send, recv, sems, early):
    for dx, dy, dz, dc in offsets:
        late = torus.late[0][dx] + torus.late[1][dy] + torus.late[2][dz]

        @pl.when(late <= 3 if early else late > 3)
        def _(to=torus.at(dx, dy, dz, dc)):
            push(torus, to, send, recv, sems)


def wait_for(ref, count, sem):
    some = ref.at[pl.ds(0, count)]
    pltpu.make_async_copy(some, some, sem).wait()


def edge(side, weights, normed, keep, wide, send):
    @pl.loop(0, S // 2, unroll=UNROLL)
    def _(q):
        proj = jnp.dot(
            weights[side * 2 * CH : (side + 1) * 2 * CH, :], normed[q], preferred_element_type=F32
        )
        mask = jnp.concatenate([keep[pl.ds(2 * q, 1), :], keep[pl.ds(2 * q + 1, 1), :]], axis=1)
        value = mask * (jnp.tanh(proj[0:CH]) + 1.0) * proj[CH : 2 * CH]
        for e in range(2):
            wide[pl.ds(2 * q + e, CH, stride=S), :] = value[:, e * L : (e + 1) * L]

    @pl.loop(0, CH // 16, unroll=UNROLL)
    def _(g):
        rows = pl.ds(pl.multiple_of(g * 256, 256), 256)
        send[pl.ds(g * 16, 16)] = wide[rows, :].reshape(16, S, L).astype(BF)


def gates(weights, normed, gate):
    @pl.loop(0, S // 2, unroll=UNROLL)
    def _(q):
        proj = jnp.dot(weights[4 * CH : 5 * CH, :], normed[q], preferred_element_type=F32)
        gate[q] = jnp.tanh(proj) + 1.0


def gather(recv, mat):
    for r in range(ROWS):
        for p in range(COLS // 2):
            low, high = swap_halves(recv[r * COLS + 2 * p], recv[r * COLS + 2 * p + 1])
            mat[r * 2 * S : r * 2 * S + S, p * L : (p + 1) * L] = low
            mat[r * 2 * S + S : (r + 1) * 2 * S, p * L : (p + 1) * L] = high


def turn(mat, turned):
    for m in range(4):
        for n in range(4):
            turned[n * L : (n + 1) * L, m * L : (m + 1) * L] = mat[
                m * L : (m + 1) * L, n * L : (n + 1) * L
            ].T


def outgoing(torus, odd, recv_l, lhs, rhs, send):
    planes = [torus.planes[odd], torus.planes[odd + 2]]
    for n, plane in enumerate(planes):
        for k in range(4):
            for p in range(COLS // 2):
                at = plane * 32 + k * COLS + 2 * p
                low, high = swap_halves(recv_l[at], recv_l[at + 1])
                row = n * L + k * 2 * S
                lhs[row : row + S, p * L : (p + 1) * L] = low
                lhs[row + S : row + 2 * S, p * L : (p + 1) * L] = high
    total = jnp.dot(lhs[...], rhs[...], preferred_element_type=F32).astype(BF)
    for n, plane in enumerate(planes):
        for k in range(4):
            row = n * L + k * 2 * S
            for p in range(COLS // 2):
                cols = slice(p * L, (p + 1) * L)
                low, high = swap_halves(total[row : row + S, cols], total[row + S : row + 2 * S, cols])
                at = plane * 32 + k * COLS + 2 * p
                send[at] = low
                send[at + 1] = high


def incoming(torus, odd, recv_r, lhs, rhs, send):
    for r in range(ROWS):
        for n in range(2):
            at = r * COLS + torus.xs[odd + 2 * n]
            low, high = swap_halves(recv_r[at], recv_r[at + 1])
            rhs[r * 2 * S : r * 2 * S + S, n * L : (n + 1) * L] = low
            rhs[r * 2 * S + S : (r + 1) * 2 * S, n * L : (n + 1) * L] = high
    for m in range(2):
        total = jnp.dot(lhs[m * 256 : (m + 1) * 256, :], rhs[...], preferred_element_type=F32).astype(BF)
        for k in range(8):
            for n in range(2):
                cols = slice(n * L, (n + 1) * L)
                low, high = swap_halves(
                    total[k * 2 * S : k * 2 * S + S, cols], total[k * 2 * S + S : (k + 1) * 2 * S, cols]
                )
                at = (m * 8 + k) * COLS + torus.xs[odd + 2 * n]
                send[at] = low
                send[at + 1] = high


def spread(recv, starts, count, wide, shift):
    total = jnp.zeros((S, L), F32)
    square = jnp.zeros((S, L), F32)
    for at in starts:
        tiles = recv[pl.ds(at, count)].astype(F32)
        wide[pl.ds(pl.multiple_of(at * S, count * S), count * S), :] = tiles.reshape(count * S, L)
        if shift is not None:
            tiles = tiles - shift[None]
            square = square + jnp.sum(tiles * tiles, axis=0)
        total = total + jnp.sum(tiles, axis=0)
    mean = total * (2.0 / CH)
    if shift is None:
        for at in starts:
            tiles = recv[pl.ds(at, count)].astype(F32) - mean[None]
            square = square + jnp.sum(tiles * tiles, axis=0)
    return mean, square


def z_starts(torus, odd):
    return [torus.planes[odd + 2 * n] * 32 + k * 16 for n in range(2) for k in range(2)]


def x_starts(torus, odd):
    return [r * COLS + torus.xs[odd + 2 * n] for r in range(ROWS) for n in range(2)]


def statistics(torus, axis, recv, sems, wide, stats):
    starts, count = (z_starts, 16) if axis == 2 else (x_starts, 2)
    wait_for(recv, len(half(axis, 0)), sems[0][1])
    mean, square = spread(recv, starts(torus, 0), count, wide, None)
    wait_for(recv, len(half(axis, 1)), sems[1][1])
    apart, more = spread(recv, starts(torus, 1), count, wide, mean)
    spread_all = (square + more - (CH / 4.0) * apart * apart) * (1.0 / CH)
    stats[0] = mean + 0.5 * apart
    stats[1] = lax.rsqrt(spread_all + 1e-05)


def finish(q, wide, stats, weights, gate, base):
    shaped = []
    for s in (2 * q, 2 * q + 1):
        row = pl.ds(s, 1)
        shaped.append((wide[pl.ds(s, CH, stride=S), :] - stats[0, row, :]) * stats[1, row, :])
    shaped = jnp.concatenate(shaped, axis=1).astype(BF)
    branch = jnp.dot(weights[...], shaped, preferred_element_type=F32)
    return (base[q].astype(F32) + gate[q] * branch).astype(BF)


def kernel(
    pair_hbm, mask_hbm, in1_hbm, gate1_hbm, final1_hbm, in2_hbm, gate2_hbm, final2_hbm, out,
    pair, mask, in1, gate1, final1, in2, gate2, final2, copy_sems,
    base, normed, gate, wide, wide2, wt, ft, keep, stats,
    send_l1, recv_l1, send_r1, recv_r1, send_t1, recv_t1, send_l2, recv_l2, send_r2, recv_r2, send_t2, recv_t2,
    mat, turned, part_a, part_b, send_sems, recv_sems,
):
    torus = Torus()
    row, col = lax.axis_index("row"), lax.axis_index("col")
    copies = [
        pltpu.make_async_copy(src, dst, copy_sems.at[k])
        for k, (src, dst) in enumerate(
            ((pair_hbm, pair), (mask_hbm, mask), (in1_hbm, in1), (gate1_hbm, gate1), (final1_hbm, final1),
             (in2_hbm, in2), (gate2_hbm, gate2), (final2_hbm, final2))
        )
    ]
    for copy in copies:
        copy.start()

    barrier = pltpu.get_barrier_semaphore()

    @pl.loop(1, DEVS)
    def _(t):
        pl.semaphore_signal(
            barrier, inc=1, device_id=lax.rem(torus.me + t, DEVS), device_id_type=LOGICAL
        )

    for copy in copies:
        copy.wait()

    wt[0, 2 * CH : 4 * CH] = turn_half(in1[:, 2 * CH : 4 * CH])

    held = mask[...].astype(F32)
    spot = lax.broadcasted_iota(jnp.int32, (S, 512), 1)
    line = lax.broadcasted_iota(jnp.int32, (S, 512), 0)
    first = jnp.sum(jnp.where(spot == row * 32 + line, held, 0.0), axis=1, keepdims=True)
    second = jnp.sum(jnp.where(spot == row * 32 + 16 + line, held, 0.0), axis=1, keepdims=True)
    spot = lax.broadcasted_iota(jnp.int32, (L, 512), 1)
    line = lax.broadcasted_iota(jnp.int32, (L, 512), 0)
    across = jnp.sum(
        jnp.where(spot == col * 64 + lax.rem(line, 64), held, 0.0), axis=1, keepdims=True
    )
    across = jnp.broadcast_to(across, (L, L)).T[0:S]
    lane = lax.broadcasted_iota(jnp.int32, (S, L), 1)
    keep[...] = jnp.where(lane < 64, first, second) * across

    @pl.loop(0, S // 2, unroll=UNROLL)
    def _(q):
        values = jnp.concatenate(
            [pair[2 * q], pair[S + 2 * q], pair[2 * q + 1], pair[S + 2 * q + 1]], axis=0
        )
        values = values.T
        base[q] = values
        normed[q] = norm0(values.astype(F32)).astype(BF)

    edge(1, wt.at[0], normed, keep, wide, send_r1)
    pl.semaphore_wait(barrier, DEVS - 1)
    sems = [(send_sems.at[k], recv_sems.at[k]) for k in range(10)]
    exchange(torus, ORDER, send_r1, recv_r1, sems[0])
    wt[0, 0 : 2 * CH] = turn_half(in1[:, 0 : 2 * CH])
    edge(0, wt.at[0], normed, keep, wide, send_l1)
    for odd in range(2):
        exchange(torus, half(2, odd), send_l1, recv_l1, sems[1 + odd])
    recv_r1[torus.me] = send_r1[torus.me]
    recv_l1[torus.me] = send_l1[torus.me]

    wt[0, 4 * CH : 5 * CH] = turn_half(gate1[...])
    wt[1, 0 : 4 * CH] = turn_half(in2[...])
    wt[1, 4 * CH : 5 * CH] = turn_half(gate2[...])
    ft[0] = turn_half(final1[...])
    ft[1] = turn_half(final2[...])
    gates(wt.at[0], normed, gate)

    wait_for(recv_r1, DEVS - 1, sems[0][1])
    gather(recv_r1, mat)
    turn(mat, turned)
    for odd in range(2):
        wait_for(recv_l1, len(half(2, odd)), sems[1 + odd][1])
        outgoing(torus, odd, recv_l1, (part_a, part_b)[odd], turned, send_t1)
        exchange(torus, half(2, odd), send_t1, recv_t1, sems[3 + odd])
    recv_t1[torus.me] = send_t1[torus.me]
    statistics(torus, 2, recv_t1, sems[3:5], wide, stats)

    @pl.loop(0, S // 2, unroll=UNROLL)
    def _(q):
        middle = finish(q, wide, stats, ft.at[0], gate, base)
        base[q] = middle
        normed[q] = norm0(middle.astype(F32)).astype(BF)

    edge(0, wt.at[1], normed, keep, wide2, send_l2)
    exchange(torus, ORDER, send_l2, recv_l2, sems[5])
    edge(1, wt.at[1], normed, keep, wide, send_r2)
    for odd in range(2):
        exchange(torus, half(0, odd), send_r2, recv_r2, sems[6 + odd])
    recv_l2[torus.me] = send_l2[torus.me]
    recv_r2[torus.me] = send_r2[torus.me]

    gates(wt.at[1], normed, gate)

    wait_for(recv_l2, DEVS - 1, sems[5][1])
    gather(recv_l2, mat)
    turn(mat, turned)
    for odd in range(2):
        wait_for(recv_r2, len(half(0, odd)), sems[6 + odd][1])
        incoming(torus, odd, recv_r2, turned, (mat.at[:, 0:256], mat.at[:, 256:512])[odd], send_t2)
        exchange_some(torus, half(0, odd), send_t2, recv_t2, sems[8 + odd], True)
    for odd in range(2):
        exchange_some(torus, half(0, odd), send_t2, recv_t2, sems[8 + odd], False)
    recv_t2[torus.me] = send_t2[torus.me]
    statistics(torus, 0, recv_t2, sems[8:10], wide, stats)

    @pl.loop(0, S // 2, unroll=UNROLL)
    def _(q):
        done = finish(q, wide, stats, ft.at[1], gate, base).T
        out[2 * q] = done[0:64]
        out[S + 2 * q] = done[64:128]
        out[2 * q + 1] = done[128:192]
        out[S + 2 * q + 1] = done[192:256]

    for k, ref in ((0, send_r1), (5, send_l2)):
        wait_for(ref, DEVS - 1, sems[k][0])
    for k, ref in ((1, send_l1), (3, send_t1), (6, send_r2), (8, send_t2)):
        for odd in range(2):
            wait_for(ref, len(half(0, odd)), sems[k + odd][0])


def shards(*args):
    pair, mask, *weights = args
    operands = (pair, mask.reshape(1, 512), *weights)
    operands = [pltpu.with_memory_space_constraint(v, pltpu.HBM) for v in operands]
    tiles = pltpu.VMEM((DEVS, S, L), BF)
    square = pltpu.VMEM((512, 512), BF)
    return pl.pallas_call(
        kernel,
        out_shape=pltpu.VMEM(pair.shape, BF),
        in_specs=[pl.BlockSpec(memory_space=pltpu.HBM)] * 8,
        out_specs=pl.BlockSpec(memory_space=pltpu.VMEM),
        scratch_shapes=[
            *[pltpu.VMEM(v.shape, v.dtype) for v in operands],
            pltpu.SemaphoreType.DMA((8,)),
            pltpu.VMEM((S // 2, CH, 2 * L), BF),
            pltpu.VMEM((S // 2, CH, 2 * L), BF),
            pltpu.VMEM((S // 2, CH, 2 * L), F32),
            pltpu.VMEM((CH * S, L), F32),
            pltpu.VMEM((CH * S, L), F32),
            pltpu.VMEM((2, 5 * CH, CH), BF),
            pltpu.VMEM((2, CH, CH), BF),
            pltpu.VMEM((S, L), F32),
            pltpu.VMEM((2, S, L), F32),
            *[tiles] * 12,
            square, square,
            pltpu.VMEM((256, 512), BF),
            pltpu.VMEM((256, 512), BF),
            pltpu.SemaphoreType.DMA((10,)),
            pltpu.SemaphoreType.DMA((10,)),
        ],
        compiler_params=pltpu.CompilerParams(
            collective_id=0, has_side_effects=True, vmem_limit_bytes=VMEM_BYTES
        ),
    )(*operands)


def solution(mesh):
    return jax.shard_map(
        shards,
        mesh=mesh,
        in_specs=(P("row", "col", None), P(), P(), P(), P(), P(), P(), P()),
        out_specs=P("row", "col", None),
        check_vma=False,
    )
```

```python
import jax
import jax.numpy as jnp
from jax import lax
from jax.experimental import pallas as pl
from jax.experimental.pallas import tpu as pltpu
from jax.sharding import PartitionSpec as P

VMEM_BYTES = 32 * 2**20
UNROLL = True
LOGICAL = pl.DeviceIdType.LOGICAL
CH = 128
S = 16
L = 128
DEVS = 128
ROWS = 16
COLS = 8
BF = jnp.bfloat16
F32 = jnp.float32
ORDER = sorted(
    ((dx, dy, dz, dc) for dz in range(4) for dy in range(4) for dx in range(4) for dc in range(2)),
    key=lambda o: -sum(min(v, 4 - v) for v in o[:3]),
)
ORDER.remove((0, 0, 0, 0))


def half(axis, odd):
    return [o for o in ORDER if o[axis] % 2 == odd]


class Torus:
    def __init__(self):
        row, col = lax.axis_index("row"), lax.axis_index("col")
        self.me = row * COLS + col
        self.z = row // 4
        y = lax.rem(col, 2) * 2 + lax.rem(row // 2, 2)
        self.planes = [lax.rem(self.z + d, 4) for d in range(4)]
        columns = [lax.rem(col // 2 + d, 4) for d in range(4)]
        ys = [lax.rem(y + d, 4) for d in range(4)]
        self.ys = [lax.rem(v, 2) * 16 + v // 2 for v in ys]
        self.xs = [v * 2 for v in columns]
        self.cs = [lax.rem(lax.rem(row, 2) + d, 2) * 8 for d in range(2)]

        self.late = ([jnp.minimum(v, 2) for v in columns], [jnp.minimum(v, 2) for v in ys], self.planes)

    def at(self, dx, dy, dz, dc):
        return self.planes[dz] * 32 + self.ys[dy] + self.xs[dx] + self.cs[dc]


def turn_half(weights):
    return (weights.astype(F32) * 0.5).astype(BF).T


def norm0(v):
    center = v - jnp.mean(v, axis=0, keepdims=True)
    spread = jnp.mean(center * center, axis=0, keepdims=True)
    return center * lax.rsqrt(spread + 1e-05)


def swap_halves(first, second):
    low = lax.broadcasted_iota(jnp.int32, first.shape, 1) < 64
    return (
        jnp.where(low, first, pltpu.roll(second, 64, 1)),
        jnp.where(low, pltpu.roll(first, 64, 1), second),
    )


def push(torus, to, send, recv, sems):
    pltpu.make_async_remote_copy(
        src_ref=send.at[to],
        dst_ref=recv.at[torus.me],
        send_sem=sems[0],
        recv_sem=sems[1],
        device_id=to,
        device_id_type=LOGICAL,
    ).start()


def exchange(torus, offsets, send, recv, sems):
    for offset in offsets:
        push(torus, torus.at(*offset), send, recv, sems)


def exchange_some(torus, offsets, send, recv, sems, early):
    for dx, dy, dz, dc in offsets:
        late = torus.late[0][dx] + torus.late[1][dy] + torus.late[2][dz]

        @pl.when(late <= 3 if early else late > 3)
        def _(to=torus.at(dx, dy, dz, dc)):
            push(torus, to, send, recv, sems)


def wait_for(ref, count, sem):
    some = ref.at[pl.ds(0, count)]
    pltpu.make_async_copy(some, some, sem).wait()


def edge(side, weights, normed, keep, wide, send):
    @pl.loop(0, S // 2, unroll=UNROLL)
    def _(q):
        proj = jnp.dot(
            weights[side * 2 * CH : (side + 1) * 2 * CH, :], normed[q], preferred_element_type=F32
        )
        mask = jnp.concatenate([keep[pl.ds(2 * q, 1), :], keep[pl.ds(2 * q + 1, 1), :]], axis=1)
        value = mask * (jnp.tanh(proj[0:CH]) + 1.0) * proj[CH : 2 * CH]
        for e in range(2):
            wide[pl.ds(2 * q + e, CH, stride=S), :] = value[:, e * L : (e + 1) * L]

    @pl.loop(0, CH // 16, unroll=UNROLL)
    def _(g):
        rows = pl.ds(pl.multiple_of(g * 256, 256), 256)
        send[pl.ds(g * 16, 16)] = wide[rows, :].reshape(16, S, L).astype(BF)


def gates(weights, normed, gate):
    @pl.loop(0, S // 2, unroll=UNROLL)
    def _(q):
        proj = jnp.dot(weights[4 * CH : 5 * CH, :], normed[q], preferred_element_type=F32)
        gate[q] = jnp.tanh(proj) + 1.0


def gather(recv, mat):
    for r in range(ROWS):
        for p in range(COLS // 2):
            low, high = swap_halves(recv[r * COLS + 2 * p], recv[r * COLS + 2 * p + 1])
            mat[r * 2 * S : r * 2 * S + S, p * L : (p + 1) * L] = low
            mat[r * 2 * S + S : (r + 1) * 2 * S, p * L : (p + 1) * L] = high


def turn(mat, turned):
    for m in range(4):
        for n in range(4):
            turned[n * L : (n + 1) * L, m * L : (m + 1) * L] = mat[
                m * L : (m + 1) * L, n * L : (n + 1) * L
            ].T


def outgoing(torus, odd, recv_l, lhs, rhs, send):
    planes = [torus.planes[odd], torus.planes[odd + 2]]
    for n, plane in enumerate(planes):
        for k in range(4):
            for p in range(COLS // 2):
                at = plane * 32 + k * COLS + 2 * p
                low, high = swap_halves(recv_l[at], recv_l[at + 1])
                row = n * L + k * 2 * S
                lhs[row : row + S, p * L : (p + 1) * L] = low
                lhs[row + S : row + 2 * S, p * L : (p + 1) * L] = high
    total = jnp.dot(lhs[...], rhs[...], preferred_element_type=F32).astype(BF)
    for n, plane in enumerate(planes):
        for k in range(4):
            row = n * L + k * 2 * S
            for p in range(COLS // 2):
                cols = slice(p * L, (p + 1) * L)
                low, high = swap_halves(total[row : row + S, cols], total[row + S : row + 2 * S, cols])
                at = plane * 32 + k * COLS + 2 * p
                send[at] = low
                send[at + 1] = high


def incoming(torus, odd, recv_r, lhs, rhs, send):
    for r in range(ROWS):
        for n in range(2):
            at = r * COLS + torus.xs[odd + 2 * n]
            low, high = swap_halves(recv_r[at], recv_r[at + 1])
            rhs[r * 2 * S : r * 2 * S + S, n * L : (n + 1) * L] = low
            rhs[r * 2 * S + S : (r + 1) * 2 * S, n * L : (n + 1) * L] = high
    for m in range(2):
        total = jnp.dot(lhs[m * 256 : (m + 1) * 256, :], rhs[...], preferred_element_type=F32).astype(BF)
        for k in range(8):
            for n in range(2):
                cols = slice(n * L, (n + 1) * L)
                low, high = swap_halves(
                    total[k * 2 * S : k * 2 * S + S, cols], total[k * 2 * S + S : (k + 1) * 2 * S, cols]
                )
                at = (m * 8 + k) * COLS + torus.xs[odd + 2 * n]
                send[at] = low
                send[at + 1] = high


def spread(recv, starts, count, wide, shift):
    total = jnp.zeros((S, L), F32)
    square = jnp.zeros((S, L), F32)
    for at in starts:
        tiles = recv[pl.ds(at, count)].astype(F32)
        wide[pl.ds(pl.multiple_of(at * S, count * S), count * S), :] = tiles.reshape(count * S, L)
        if shift is not None:
            tiles = tiles - shift[None]
            square = square + jnp.sum(tiles * tiles, axis=0)
        total = total + jnp.sum(tiles, axis=0)
    mean = total * (2.0 / CH)
    if shift is None:
        for at in starts:
            tiles = recv[pl.ds(at, count)].astype(F32) - mean[None]
            square = square + jnp.sum(tiles * tiles, axis=0)
    return mean, square


def z_starts(torus, odd):
    return [torus.planes[odd + 2 * n] * 32 + k * 16 for n in range(2) for k in range(2)]


def x_starts(torus, odd):
    return [r * COLS + torus.xs[odd + 2 * n] for r in range(ROWS) for n in range(2)]


def statistics(torus, axis, recv, sems, wide, stats):
    starts, count = (z_starts, 16) if axis == 2 else (x_starts, 2)
    wait_for(recv, len(half(axis, 0)), sems[0][1])
    mean, square = spread(recv, starts(torus, 0), count, wide, None)
    wait_for(recv, len(half(axis, 1)), sems[1][1])
    apart, more = spread(recv, starts(torus, 1), count, wide, mean)
    spread_all = (square + more - (CH / 4.0) * apart * apart) * (1.0 / CH)
    stats[0] = mean + 0.5 * apart
    stats[1] = lax.rsqrt(spread_all + 1e-05)


def finish(q, wide, stats, weights, gate, base):
    shaped = []
    for s in (2 * q, 2 * q + 1):
        row = pl.ds(s, 1)
        shaped.append((wide[pl.ds(s, CH, stride=S), :] - stats[0, row, :]) * stats[1, row, :])
    shaped = jnp.concatenate(shaped, axis=1).astype(BF)
    branch = jnp.dot(weights[...], shaped, preferred_element_type=F32)
    return (base[q].astype(F32) + gate[q] * branch).astype(BF)


def kernel(
    pair_hbm, mask_hbm, in1_hbm, gate1_hbm, final1_hbm, in2_hbm, gate2_hbm, final2_hbm, out,
    pair, mask, in1, gate1, final1, in2, gate2, final2, copy_sems,
    base, normed, gate, wide, wide2, wt, ft, keep, stats,
    send_l1, recv_l1, send_r1, recv_r1, send_t1, recv_t1, send_l2, recv_l2, send_r2, recv_r2, send_t2, recv_t2,
    mat, turned, part_a, part_b, send_sems, recv_sems,
):
    torus = Torus()
    row, col = lax.axis_index("row"), lax.axis_index("col")
    copies = [
        pltpu.make_async_copy(src, dst, copy_sems.at[k])
        for k, (src, dst) in enumerate(
            ((pair_hbm, pair), (mask_hbm, mask), (in1_hbm, in1), (gate1_hbm, gate1), (final1_hbm, final1),
             (in2_hbm, in2), (gate2_hbm, gate2), (final2_hbm, final2))
        )
    ]
    for copy in copies:
        copy.start()

    barrier = pltpu.get_barrier_semaphore()

    for offset in ORDER:
        pl.semaphore_signal(barrier, inc=1, device_id=torus.at(*offset), device_id_type=LOGICAL)

    for copy in copies:
        copy.wait()

    wt[0, 2 * CH : 4 * CH] = turn_half(in1[:, 2 * CH : 4 * CH])

    held = mask[...].astype(F32)
    spot = lax.broadcasted_iota(jnp.int32, (S, 512), 1)
    line = lax.broadcasted_iota(jnp.int32, (S, 512), 0)
    first = jnp.sum(jnp.where(spot == row * 32 + line, held, 0.0), axis=1, keepdims=True)
    second = jnp.sum(jnp.where(spot == row * 32 + 16 + line, held, 0.0), axis=1, keepdims=True)
    spot = lax.broadcasted_iota(jnp.int32, (L, 512), 1)
    line = lax.broadcasted_iota(jnp.int32, (L, 512), 0)
    across = jnp.sum(
        jnp.where(spot == col * 64 + lax.rem(line, 64), held, 0.0), axis=1, keepdims=True
    )
    across = jnp.broadcast_to(across, (L, L)).T[0:S]
    lane = lax.broadcasted_iota(jnp.int32, (S, L), 1)
    keep[...] = jnp.where(lane < 64, first, second) * across

    @pl.loop(0, S // 2, unroll=UNROLL)
    def _(q):
        values = jnp.concatenate(
            [pair[2 * q], pair[S + 2 * q], pair[2 * q + 1], pair[S + 2 * q + 1]], axis=0
        )
        values = values.T
        base[q] = values
        normed[q] = norm0(values.astype(F32)).astype(BF)

    edge(1, wt.at[0], normed, keep, wide, send_r1)
    pl.semaphore_wait(barrier, DEVS - 1)
    sems = [(send_sems.at[k], recv_sems.at[k]) for k in range(10)]
    exchange(torus, ORDER, send_r1, recv_r1, sems[0])
    wt[0, 0 : 2 * CH] = turn_half(in1[:, 0 : 2 * CH])
    edge(0, wt.at[0], normed, keep, wide, send_l1)
    for odd in range(2):
        exchange(torus, half(2, odd), send_l1, recv_l1, sems[1 + odd])
    recv_r1[torus.me] = send_r1[torus.me]
    recv_l1[torus.me] = send_l1[torus.me]

    wt[0, 4 * CH : 5 * CH] = turn_half(gate1[...])
    wt[1, 0 : 4 * CH] = turn_half(in2[...])
    wt[1, 4 * CH : 5 * CH] = turn_half(gate2[...])
    ft[0] = turn_half(final1[...])
    ft[1] = turn_half(final2[...])
    gates(wt.at[0], normed, gate)

    wait_for(recv_r1, DEVS - 1, sems[0][1])
    gather(recv_r1, mat)
    turn(mat, turned)
    for odd in range(2):
        wait_for(recv_l1, len(half(2, odd)), sems[1 + odd][1])
        outgoing(torus, odd, recv_l1, (part_a, part_b)[odd], turned, send_t1)
        exchange(torus, half(2, odd), send_t1, recv_t1, sems[3 + odd])
    recv_t1[torus.me] = send_t1[torus.me]
    statistics(torus, 2, recv_t1, sems[3:5], wide, stats)

    @pl.loop(0, S // 2, unroll=UNROLL)
    def _(q):
        middle = finish(q, wide, stats, ft.at[0], gate, base)
        base[q] = middle
        normed[q] = norm0(middle.astype(F32)).astype(BF)

    edge(0, wt.at[1], normed, keep, wide2, send_l2)
    exchange(torus, ORDER, send_l2, recv_l2, sems[5])
    edge(1, wt.at[1], normed, keep, wide, send_r2)
    for odd in range(2):
        exchange(torus, half(0, odd), send_r2, recv_r2, sems[6 + odd])
    recv_l2[torus.me] = send_l2[torus.me]
    recv_r2[torus.me] = send_r2[torus.me]

    gates(wt.at[1], normed, gate)

    wait_for(recv_l2, DEVS - 1, sems[5][1])
    gather(recv_l2, mat)
    turn(mat, turned)
    for odd in range(2):
        wait_for(recv_r2, len(half(0, odd)), sems[6 + odd][1])
        incoming(torus, odd, recv_r2, turned, (mat.at[:, 0:256], mat.at[:, 256:512])[odd], send_t2)
        exchange_some(torus, half(0, odd), send_t2, recv_t2, sems[8 + odd], True)
    for odd in range(2):
        exchange_some(torus, half(0, odd), send_t2, recv_t2, sems[8 + odd], False)
    recv_t2[torus.me] = send_t2[torus.me]
    statistics(torus, 0, recv_t2, sems[8:10], wide, stats)

    @pl.loop(0, S // 2, unroll=UNROLL)
    def _(q):
        done = finish(q, wide, stats, ft.at[1], gate, base).T
        out[2 * q] = done[0:64]
        out[S + 2 * q] = done[64:128]
        out[2 * q + 1] = done[128:192]
        out[S + 2 * q + 1] = done[192:256]

    for k, ref in ((0, send_r1), (5, send_l2)):
        wait_for(ref, DEVS - 1, sems[k][0])
    for k, ref in ((1, send_l1), (3, send_t1), (6, send_r2), (8, send_t2)):
        for odd in range(2):
            wait_for(ref, len(half(0, odd)), sems[k + odd][0])


def shards(*args):
    pair, mask, *weights = args
    operands = (pair, mask.reshape(1, 512), *weights)
    operands = [pltpu.with_memory_space_constraint(v, pltpu.HBM) for v in operands]
    tiles = pltpu.VMEM((DEVS, S, L), BF)
    square = pltpu.VMEM((512, 512), BF)
    return pl.pallas_call(
        kernel,
        out_shape=pltpu.VMEM(pair.shape, BF),
        in_specs=[pl.BlockSpec(memory_space=pltpu.HBM)] * 8,
        out_specs=pl.BlockSpec(memory_space=pltpu.VMEM),
        scratch_shapes=[
            *[pltpu.VMEM(v.shape, v.dtype) for v in operands],
            pltpu.SemaphoreType.DMA((8,)),
            pltpu.VMEM((S // 2, CH, 2 * L), BF),
            pltpu.VMEM((S // 2, CH, 2 * L), BF),
            pltpu.VMEM((S // 2, CH, 2 * L), F32),
            pltpu.VMEM((CH * S, L), F32),
            pltpu.VMEM((CH * S, L), F32),
            pltpu.VMEM((2, 5 * CH, CH), BF),
            pltpu.VMEM((2, CH, CH), BF),
            pltpu.VMEM((S, L), F32),
            pltpu.VMEM((2, S, L), F32),
            *[tiles] * 12,
            square, square,
            pltpu.VMEM((256, 512), BF),
            pltpu.VMEM((256, 512), BF),
            pltpu.SemaphoreType.DMA((10,)),
            pltpu.SemaphoreType.DMA((10,)),
        ],
        compiler_params=pltpu.CompilerParams(
            collective_id=0, has_side_effects=True, vmem_limit_bytes=VMEM_BYTES
        ),
    )(*operands)


def solution(mesh):
    return jax.shard_map(
        shards,
        mesh=mesh,
        in_specs=(P("row", "col", None), P(), P(), P(), P(), P(), P(), P()),
        out_specs=P("row", "col", None),
        check_vma=False,
    )
```
